32 devices in a mesh: section: 4 (over y, core), fsdp: 8 (over z, x).
Axes of the slice: x: 2, y: 2, z: 4, core: 2. Of those that a mesh axis runs over, the one named last changes fastest.
Arguments:
- layer_input: bfloat16 [4, 4096, 2048], P('section', 'fsdp'), may hold values from -6 to 6
- resid_grad: bfloat16 [4, 4096, 2048], P('section', 'fsdp'), may hold values from -6 to 6
- qkv_grad: bfloat16 [4, 4096, 3072], P('section', 'fsdp'), may hold values from -6 to 6
- prev_input: bfloat16 [4, 4096, 2048], P('section', 'fsdp'), may hold values from -6 to 6
- prev_qkv_grad: bfloat16 [4, 4096, 3072], P('section', 'fsdp'), may hold values from -0.059814453 to 0.059814453
- qkv_weight: bfloat16 [4, 2048, 3072], P('section', 'fsdp'), may hold values from -0.125 to 0.125
- norm_gain: float32 [4, 2048], P('section'), may hold values from 0.1 to 1.9
Outputs:
- upstream_grad: bfloat16 [4, 4096, 2048], P('section', 'fsdp')
- weight_grad: float32 [4, 2048, 3072], P('section', 'fsdp')
- gain_grad: float32 [4, 2048], P('section')
The draws below stay inside these ranges and needn't reach their ends.
All inputs are finite; a program needn't handle non-finite values.
Results may differ from the reference program's by a relative error of at most 0.018.
Values may be sent and summed in bfloat16 or wider, within the bound.
No kernel may reach another device: no remote copies, remote signals or barrier semaphores. Data moves between devices by JAX's collectives and lax.ppermute only.
A program may use at most 128 MiB of HBM per device.

```python
import jax
import jax.numpy as jnp
from jax import lax

D = 2048
TOK_DEV = 512
QKV = 3072
TOKENS = 4096
N_SECTION = 4
N_FSDP = 8


def spiked(values, key, source, target, blocks, factor):
    owner, partner = [(jnp.arange(values.shape[position]) // (values.shape[position] // blocks)).reshape([-1 if axis == position else 1 for axis in range(values.ndim)]) for position in (source, target)]
    chosen = jax.random.permutation(key, blocks)[partner]
    strong = (owner == chosen) | (owner == (partner + blocks // 2) % blocks)
    return jnp.where(strong, factor * values, values)


def level_of(rng, extent, shards, least, largest):
    def one(axis_at, shards_of):
        steps = jax.random.uniform(jax.random.fold_in(jax.random.fold_in(rng, 6), axis_at), (shards_of,), jnp.float32, least / len(shards), largest / len(shards))
        return jnp.repeat(jnp.exp(steps), extent[axis_at] // shards_of).reshape((-1,) + (1,) * (len(extent) - axis_at - 1))

    factor_of = one(*shards[0])
    for cut in shards[1:]:
        factor_of = factor_of * one(*cut)
    return factor_of


def noise(own_key, shape, deviation, most, shards=(), held_as=jnp.bfloat16):
    array = jax.random.normal(own_key, shape, jnp.float32) * deviation
    if len(shards) > 0:
        array = level_of(own_key, shape, shards, -0.22, 0.18) * array
    return jnp.clip(array, min=-most, max=most).astype(held_as)


def bell_draw_with(stream_key, dims, scale, most, cuts, heavy, dtype=jnp.bfloat16):
    drawn = scale * jax.random.normal(stream_key, dims, jnp.float32)
    if cuts:
        drawn = drawn * level_of(stream_key, dims, cuts, -0.22, 0.18)
    return jnp.clip(spiked(drawn, jax.random.fold_in(stream_key, 3), *heavy), -most, most).astype(dtype)


def setup_inputs(seed: int = 0) -> dict:
    seeds = jax.random.split(jax.random.key(seed), 8)
    return {
        "layer_input": noise(seeds[0], (N_SECTION, TOKENS, D), 1.0, 6.0, ((0, 4), (1, 8))),
        "resid_grad": noise(seeds[1], (N_SECTION, TOKENS, D), 1.0, 6.0, ((0, 4), (1, 8))),
        "qkv_grad": noise(seeds[2], (N_SECTION, TOKENS, QKV), 1.0, 6.0, ((0, 4), (1, 8))),
        "prev_input": bell_draw_with(seeds[3], (N_SECTION, TOKENS, D), 1.0, 6.0, ((0, 4), (1, 8)), (1, 2, 8, 2.0)),
        "prev_qkv_grad": noise(seeds[4], (N_SECTION, TOKENS, QKV), 0.01, 0.059814453, ((0, 4), (1, 8))),
        "qkv_weight": noise(seeds[5], (N_SECTION, D, QKV), D ** -0.5, 0.125, ((0, 4), (1, 8))),
        "norm_gain": jnp.clip(1.0 + 0.18 * jax.random.normal(seeds[6], (N_SECTION, D), jnp.float32), 0.1, 1.9),
    }


EPS = 1e-05

def row_scale(rows):
    values = rows.astype(jnp.float32)
    return lax.rsqrt(lax.optimization_barrier(jnp.mean(values * values, axis=-1, keepdims=True)) + EPS)

def transpose_product(grads, weight):
    return lax.dot_general(grads, weight, (((1,), (1,)), ((), ())), preferred_element_type=jnp.float32)

def input_backward(rows, resid, grads, weight, gain):
    direction = transpose_product(grads, weight)
    scale = row_scale(rows)
    values = rows.astype(jnp.float32)
    gained = gain[None, :] * direction
    inner = lax.optimization_barrier(jnp.mean(gained * values, axis=-1, keepdims=True))
    result = resid.astype(jnp.float32) + scale * gained - values * scale * scale * scale * inner
    return result.astype(jnp.bfloat16)

def weight_backward(rows, grads, gain):
    scale = row_scale(rows)
    normed = (rows.astype(jnp.float32) * scale * gain[None, :]).astype(jnp.bfloat16)
    normed_blocks = normed.reshape(N_FSDP, TOK_DEV, normed.shape[1])
    grad_blocks = grads.reshape(N_FSDP, TOK_DEV, grads.shape[1])

    def add_block(total, pair):
        term = lax.dot_general(pair[0], pair[1], (((0,), (0,)), ((), ())), preferred_element_type=jnp.float32)
        rounded = lax.optimization_barrier(term.astype(jnp.bfloat16))
        return (total + rounded.astype(jnp.float32), None)
    start = jnp.zeros((normed.shape[1], grads.shape[1]), jnp.float32)
    total, unused = lax.scan(add_block, start, (normed_blocks, grad_blocks))
    return total

def gain_backward(weight_total, weight, gain):
    return lax.optimization_barrier(jnp.sum(weight.astype(jnp.float32) * weight_total, axis=1)) / gain

def reference(layer_input, resid_grad, qkv_grad, prev_input, prev_qkv_grad, qkv_weight, norm_gain):
    locals_list = []
    weight_list = []
    gain_list = []
    for layer in range(N_SECTION):
        locals_list.append(input_backward(layer_input[layer], resid_grad[layer], qkv_grad[layer], qkv_weight[layer], norm_gain[layer]))
        weight_total = weight_backward(prev_input[layer], prev_qkv_grad[layer], norm_gain[layer])
        weight_list.append(weight_total)
        gain_list.append(gain_backward(weight_total, qkv_weight[layer], norm_gain[layer]))
    upstream_grad = jnp.stack(locals_list[1:] + [jnp.zeros_like(locals_list[0])])
    return (upstream_grad, jnp.stack(weight_list), jnp.stack(gain_list))
```

```python
import jax
import jax.numpy as jnp
from jax import lax
from jax.sharding import PartitionSpec as P

EPS = 1e-05
BF16 = jnp.bfloat16
F32 = jnp.float32


def row_scale(rows):
    values = rows.astype(F32)
    return lax.rsqrt(jnp.mean(values * values, axis=-1, keepdims=True) + EPS)


def after(value, earlier):
    return lax.optimization_barrier((value, earlier))[0]


def swap(value, axis):
    count = lax.axis_size(axis)
    return lax.ppermute(value, axis, [(i, i ^ 1) for i in range(count)])


def hop(value, axis, sources, step):
    return lax.ppermute(
        value, axis, [(2 * o + q, 2 * (o + step) + q) for o in sources for q in range(2)]
    )


def split_halves(array, owned):
    pieces = [array[..., i : i + owned] for i in range(0, array.shape[-1], owned)]
    return jnp.concatenate(pieces[0::2], axis=-1), jnp.concatenate(pieces[1::2], axis=-1)


def join_halves(even, odd, owned):
    pieces = []
    for i in range(0, even.shape[-1], owned):
        pieces += [even[..., i : i + owned], odd[..., i : i + owned]]
    return jnp.concatenate(pieces, axis=-1)


def gather_half(shard, axis, pairs, pair):
    owned = shard.shape[0]
    up, down = {0: shard}, {0: shard}
    for r in range(1, pairs):
        up[r] = hop(up[r - 1], axis, range(pairs - 1), 1)
        down[r] = hop(down[r - 1], axis, range(1, pairs), -1)
    full = jnp.zeros((pairs * owned, shard.shape[1]), shard.dtype)
    full = lax.dynamic_update_slice_in_dim(full, shard, pair * owned, 0)
    for j in range(1, pairs):
        block = jnp.where(pair >= j, up[j], down[pairs - j])
        full = lax.dynamic_update_slice_in_dim(full, block, lax.rem(pair - j + pairs, pairs) * owned, 0)
    return full


def scatter_sum(term, axis, pairs, pair, owned):
    def block(at):
        return lax.dynamic_slice_in_dim(term, at * owned, owned, 0)

    up = down = None
    for s in range(1, pairs):
        send_up = block(jnp.minimum(pair + pairs - s, pairs - 1))
        send_down = block(jnp.maximum(pair - pairs + s, 0))
        if s > 1:
            send_up = (send_up.astype(F32) + up.astype(F32)).astype(BF16)
            send_down = (send_down.astype(F32) + down.astype(F32)).astype(BF16)
        up = hop(send_up, axis, range(s), 1)
        down = hop(send_down, axis, range(pairs - s, pairs), -1)
    total = block(pair).astype(F32)
    if pairs > 1:
        total = total + up.astype(F32) + down.astype(F32)
    return total


def transpose_product(grads, piece):
    return lax.dot_general(grads, piece, (((1,), (1,)), ((), ())), preferred_element_type=F32)


def rows_product(rows, grads):
    return lax.dot_general(rows, grads, (((0,), (0,)), ((), ())), preferred_element_type=F32)


def gather_all(part, axis):
    count = lax.axis_size(axis)
    me = lax.axis_index(axis)
    got = [part] + [
        lax.ppermute(part, axis, [(i, (i + k) % count) for i in range(count)]) for k in range(1, count)
    ]
    stacked = jnp.stack(got)
    order = lax.rem(me - jnp.arange(count) + count, count)
    return stacked[order].reshape(-1)


def local(layer_input, resid_grad, qkv_grad, prev_input, prev_qkv_grad, qkv_weight, norm_gain):
    axis = "fsdp"
    rows_now, resid, grads_now = layer_input[0], resid_grad[0], qkv_grad[0]
    rows_prev, grads_prev = prev_input[0], prev_qkv_grad[0]
    weight_rows, gain = qkv_weight[0], norm_gain[0]
    owned, columns = weight_rows.shape
    tokens = rows_now.shape[0]
    count = lax.axis_size(axis)
    pairs = count // 2
    me = lax.axis_index(axis)
    pair, side = me // 2, lax.rem(me, 2)
    first = side == 0

    col_chunks, tok_chunks = 3, 4
    wide, tall = columns // col_chunks, tokens // tok_chunks

    weight_half = gather_half(weight_rows, axis, pairs, pair)

    window = []

    def exchange(value):
        if len(window) >= 2:
            value = after(value, window[-2])
        got = swap(value, axis)
        window.append(got)
        return got

    prev_normed = (rows_prev.astype(F32) * row_scale(rows_prev) * gain[None, :]).astype(BF16)
    even, odd = split_halves(prev_normed, owned)
    normed_mine = jnp.where(first, even, odd)
    normed_theirs = jnp.where(first, odd, even)

    prev_pieces = [grads_prev[:, i * wide : (i + 1) * wide] for i in range(col_chunks)]
    got_pieces = [exchange(prev_pieces[0])]
    normed_got = exchange(normed_theirs)
    for piece in prev_pieces[1:]:
        got_pieces.append(exchange(piece))

    now_pieces = [grads_now[i * tall : (i + 1) * tall] for i in range(tok_chunks)]
    got_now = [exchange(piece) for piece in now_pieces]

    totals = []
    for mine, theirs in zip(prev_pieces, got_pieces):
        term = (rows_product(normed_mine, mine) + rows_product(normed_got, theirs)).astype(BF16)
        totals.append(scatter_sum(term, axis, pairs, pair, owned))
    weight_grad = jnp.concatenate(totals, axis=1)
    owned_gain = lax.dynamic_slice_in_dim(gain, me * owned, owned, 0)
    gain_part = jnp.sum(weight_rows.astype(F32) * weight_grad, axis=1) / owned_gain
    gain_grad = gather_all(gain_part, axis)

    upstream = []
    layers = lax.axis_size("section")
    for i in range(tok_chunks):
        back = swap(transpose_product(got_now[i], weight_half).astype(BF16), axis)
        mine = transpose_product(now_pieces[i], weight_half)
        theirs = back.astype(F32)
        direction = join_halves(jnp.where(first, mine, theirs), jnp.where(first, theirs, mine), owned)
        rows = slice(i * tall, (i + 1) * tall)
        values = rows_now[rows].astype(F32)
        scale = row_scale(rows_now[rows])
        gained = gain[None, :] * direction
        inner = jnp.mean(gained * values, axis=-1, keepdims=True)
        local_grad = (
            resid[rows].astype(F32) + scale * gained - values * scale * scale * scale * inner
        ).astype(BF16)
        upstream.append(lax.ppermute(local_grad, "section", [(k + 1, k) for k in range(layers - 1)]))
    upstream_grad = jnp.concatenate(upstream, axis=0)
    return (upstream_grad[None], weight_grad[None], gain_grad[None])


def solution(mesh):
    placed = (
        P("section", "fsdp", None),
        P("section", "fsdp", None),
        P("section", "fsdp", None),
        P("section", "fsdp", None),
        P("section", "fsdp", None),
        P("section", "fsdp", None),
        P("section", None),
    )
    return jax.shard_map(
        local,
        mesh=mesh,
        in_specs=placed,
        out_specs=(P("section", "fsdp", None), P("section", "fsdp", None), P("section", None)),
        check_vma=False,
    )
```

```python
import math

import jax
import jax.numpy as jnp
from jax import lax
from jax.experimental import pallas as pl
from jax.experimental.pallas import tpu as pltpu
from jax.sharding import PartitionSpec as P

EPS = 1e-05
BF16 = jnp.bfloat16
F32 = jnp.float32


def row_scale(rows):
    values = rows.astype(F32)
    return lax.rsqrt(jnp.mean(values * values, axis=-1, keepdims=True) + EPS)


def swap(value, axis):
    count = lax.axis_size(axis)
    return lax.ppermute(value, axis, [(i, i ^ 1) for i in range(count)])


def hop(value, axis, sources, step):
    return lax.ppermute(
        value, axis, [(2 * o + q, 2 * (o + step) + q) for o in sources for q in range(2)]
    )


def split_halves(array, owned):
    pieces = [array[..., i : i + owned] for i in range(0, array.shape[-1], owned)]
    return jnp.concatenate(pieces[0::2], axis=-1), jnp.concatenate(pieces[1::2], axis=-1)


def join_halves(even, odd, owned):
    pieces = []
    for i in range(0, even.shape[-1], owned):
        pieces += [even[..., i : i + owned], odd[..., i : i + owned]]
    return jnp.concatenate(pieces, axis=-1)


class Gather:
    def __init__(self, shard, axis, pairs, pair):
        self.shard, self.axis, self.pairs, self.pair = shard, axis, pairs, pair
        self.ups, self.downs, self.flying = [], [], []
        self.advance()

    def advance(self):
        if self.flying:
            self.ups.append(self.flying[0])
            self.downs.append(self.flying[1])
        r = len(self.ups) + 1
        up = hop(([self.shard] + self.ups)[-1], self.axis, range(r - 1, self.pairs - 1), 1)
        down = hop(([self.shard] + self.downs)[-1], self.axis, range(1, self.pairs - r + 1), -1)
        self.flying = [up, down]

    def done(self):
        return len(self.ups) == self.pairs - 2

    def whole(self):
        return assemble(self.pair, self.shard, self.ups + self.flying[:1], self.downs + self.flying[1:])


class Scatter:
    def __init__(self, term, axis, pairs, pair, owned):
        self.term, self.axis, self.pairs, self.pair, self.owned = term, axis, pairs, pair, owned
        self.step, self.flying = 0, []
        self.advance()

    def advance(self):
        self.step += 1
        s, pairs, pair = self.step, self.pairs, self.pair
        above = jnp.minimum(pair + pairs - s, pairs - 1)
        below = jnp.maximum(pair - pairs + s, 0)
        if s == 1 and pairs >= 4:
            (send,) = pick_and_add(self.term, [jnp.where(pair < pairs // 2, above, below)], [], self.owned)
            route = [(q, 2 + q) for q in range(2)]
            route += [(2 * pairs - 2 + q, 2 * pairs - 4 + q) for q in range(2)]
            self.flying = [lax.ppermute(send, self.axis, route)]
            return
        came = [self.flying[0], self.flying[-1]] if self.flying else []
        send_up, send_down = pick_and_add(self.term, [above, below], came, self.owned)
        self.flying = [
            hop(send_up, self.axis, range(s), 1),
            hop(send_down, self.axis, range(pairs - s, pairs), -1),
        ]

    def done(self):
        return self.step == self.pairs - 1

    def total(self):
        own = lax.dynamic_slice_in_dim(self.term, self.pair * self.owned, self.owned, 0)
        return own.astype(F32) + sum(came.astype(F32) for came in self.flying)


SMALL = pl.CostEstimate(flops=1, bytes_accessed=1, transcendentals=0)
PARAMS = pltpu.CompilerParams(vmem_limit_bytes=48 * 1024 * 1024)


def assemble(pair, shard, ups, downs):
    pairs, owned = len(ups) + 1, shard.shape[0]

    def kernel(pair_ref, shard_ref, *refs):
        up_refs, down_refs = refs[: pairs - 1], refs[pairs - 1 : 2 * pairs - 2]
        out_ref, slots, came, gone = refs[2 * pairs - 2 :]
        here = pair_ref[0]

        def bring(source, at):
            return pltpu.make_async_copy(source, slots.at[at], came.at[at])

        def put(at):
            return pltpu.make_async_copy(slots.at[at], out_ref.at[pl.ds(at * owned, owned)], gone.at[at])

        for at in range(pairs):
            for source_pair in range(pairs):
                distance = source_pair - at
                if distance == 0:
                    source = shard_ref
                elif distance > 0:
                    source = up_refs[distance - 1]
                else:
                    source = down_refs[-distance - 1]

                @pl.when(here == source_pair)
                def _(source=source, at=at):
                    bring(source, at).start()

        for at in range(pairs):
            bring(shard_ref, at).wait()
            put(at).start()
        for at in range(pairs):
            put(at).wait()

    return pl.pallas_call(
        kernel,
        out_shape=jax.ShapeDtypeStruct((pairs * owned, shard.shape[1]), shard.dtype),
        in_specs=[pl.BlockSpec(memory_space=pltpu.SMEM)] + [pl.BlockSpec(memory_space=pl.ANY)] * (2 * pairs - 1),
        out_specs=pl.BlockSpec(memory_space=pl.ANY),
        scratch_shapes=[
            pltpu.VMEM((pairs,) + shard.shape, shard.dtype),
            pltpu.SemaphoreType.DMA((pairs,)),
            pltpu.SemaphoreType.DMA((pairs,)),
        ],
        compiler_params=PARAMS,
        cost_estimate=SMALL,
    )(pair.reshape(1), shard, *ups, *downs)


def first_packet(rows, gain, grads, wide, side, owned):
    tokens, features = rows.shape
    half = features // 2
    block = min(128, tokens)

    def kernel(side_ref, rows_ref, gain_ref, grads_ref, mine_ref, packet_ref):
        values = rows_ref[...].astype(F32)
        scale = lax.rsqrt(jnp.mean(values * values, axis=-1, keepdims=True) + EPS)
        normed = (values * scale * gain_ref[...]).astype(BF16)
        even, odd = split_halves(normed, owned)
        packet_ref[:, half:] = grads_ref[...]

        @pl.when(side_ref[0] == 0)
        def _():
            mine_ref[...] = even.T
            packet_ref[:, :half] = odd

        @pl.when(side_ref[0] != 0)
        def _():
            mine_ref[...] = odd.T
            packet_ref[:, :half] = even

    return pl.pallas_call(
        kernel,
        grid=(tokens // block,),
        in_specs=[
            pl.BlockSpec(memory_space=pltpu.SMEM),
            pl.BlockSpec((block, features), lambda i: (i, 0)),
            pl.BlockSpec((1, features), lambda i: (0, 0)),
            pl.BlockSpec((block, wide), lambda i: (i, 0)),
        ],
        out_specs=[
            pl.BlockSpec((half, block), lambda i: (0, i)),
            pl.BlockSpec((block, half + wide), lambda i: (i, 0)),
        ],
        out_shape=[
            jax.ShapeDtypeStruct((half, tokens), BF16),
            jax.ShapeDtypeStruct((tokens, half + wide), BF16),
        ],
        compiler_params=PARAMS,
        cost_estimate=SMALL,
    )(side.reshape(1), rows, gain[None, :], grads)


def pick_and_add(term, places, came, owned):
    wide = term.shape[1]
    block = wide // 2
    count = len(places)

    def kernel(at_ref, *refs):
        for i in range(count):
            value = refs[i][...]
            if came:
                value = (value.astype(F32) + refs[count + i][...].astype(F32)).astype(BF16)
            refs[-count + i][...] = value

    plain = pl.BlockSpec((owned, block), lambda j, at: (0, j))
    return pl.pallas_call(
        kernel,
        grid_spec=pltpu.PrefetchScalarGridSpec(
            num_scalar_prefetch=1,
            grid=(wide // block,),
            in_specs=[
                pl.BlockSpec((owned, block), lambda j, at, i=i: (at[i], j)) for i in range(count)
            ] + [plain] * len(came),
            out_specs=[plain] * count,
        ),
        out_shape=[jax.ShapeDtypeStruct((owned, wide), BF16)] * count,
        compiler_params=PARAMS,
        cost_estimate=SMALL,
    )(jnp.stack(places), *[term] * count, *came)


def transpose_product(grads, weight, dtype):
    rows, depth = grads.shape
    block = min(256, weight.shape[0])

    def kernel(grads_ref, weight_ref, out_ref, flipped):
        @pl.when(pl.program_id(0) == 0)
        def _():
            flipped[...] = grads_ref[...].T

        product = jnp.dot(weight_ref[...], flipped[...], preferred_element_type=F32)
        out_ref[...] = product.T.astype(dtype)

    return pl.pallas_call(
        kernel,
        grid=(weight.shape[0] // block,),
        in_specs=[
            pl.BlockSpec((rows, depth), lambda j: (0, 0)),
            pl.BlockSpec((block, depth), lambda j: (j, 0)),
        ],
        out_specs=pl.BlockSpec((rows, block), lambda j: (0, j)),
        out_shape=jax.ShapeDtypeStruct((rows, weight.shape[0]), dtype),
        scratch_shapes=[pltpu.VMEM((depth, rows), grads.dtype)],
        compiler_params=PARAMS,
        cost_estimate=SMALL,
    )(grads, weight)


def input_gradient(mine, theirs, start, rows, resid, gain, side, owned):
    tokens, half = theirs.shape
    features = 2 * half
    block = min(128, tokens)
    first_block = start // block

    def kernel(side_ref, mine_ref, theirs_ref, rows_ref, resid_ref, gain_ref, out_ref):
        def result(even, odd):
            values = rows_ref[...].astype(F32)
            scale = lax.rsqrt(jnp.mean(values * values, axis=-1, keepdims=True) + EPS)
            gained = gain_ref[...] * join_halves(even, odd, owned)
            inner = jnp.mean(gained * values, axis=-1, keepdims=True)
            out_ref[...] = (
                resid_ref[...].astype(F32) + scale * gained - values * (scale * scale * scale * inner)
            ).astype(BF16)

        @pl.when(side_ref[0] == 0)
        def _():
            result(mine_ref[...], theirs_ref[...].astype(F32))

        @pl.when(side_ref[0] != 0)
        def _():
            result(theirs_ref[...].astype(F32), mine_ref[...])

    return pl.pallas_call(
        kernel,
        grid=(tokens // block,),
        in_specs=[
            pl.BlockSpec(memory_space=pltpu.SMEM),
            pl.BlockSpec((block, half), lambda i: (first_block + i, 0)),
            pl.BlockSpec((block, half), lambda i: (i, 0)),
            pl.BlockSpec((block, features), lambda i: (first_block + i, 0)),
            pl.BlockSpec((block, features), lambda i: (first_block + i, 0)),
            pl.BlockSpec((1, features), lambda i: (0, 0)),
        ],
        out_specs=pl.BlockSpec((block, features), lambda i: (i, 0)),
        out_shape=jax.ShapeDtypeStruct((tokens, features), BF16),
        compiler_params=PARAMS,
        cost_estimate=SMALL,
    )(side.reshape(1), mine, theirs, rows, resid, gain[None, :])


def weight_term(mine, grads, start, packet, got, got_start):
    features, tokens = mine.shape
    wide = got.shape[1] - got_start
    block = math.gcd(math.gcd(start, wide), math.gcd(got_start, 512))
    first_block, first_got = start // block, got_start // block

    def kernel(mine_ref, grads_ref, theirs_ref, got_ref, out_ref, flipped):
        @pl.when(pl.program_id(0) == 0)
        def _():
            flipped[...] = theirs_ref[...].T

        total = jnp.dot(mine_ref[...], grads_ref[...], preferred_element_type=F32)
        total += jnp.dot(flipped[...], got_ref[...], preferred_element_type=F32)
        out_ref[...] = total.astype(BF16)

    return pl.pallas_call(
        kernel,
        grid=(wide // block,),
        in_specs=[
            pl.BlockSpec((features, tokens), lambda j: (0, 0)),
            pl.BlockSpec((tokens, block), lambda j: (0, first_block + j)),
            pl.BlockSpec((tokens, features), lambda j: (0, 0)),
            pl.BlockSpec((tokens, block), lambda j: (0, first_got + j)),
        ],
        out_specs=pl.BlockSpec((features, block), lambda j: (0, j)),
        out_shape=jax.ShapeDtypeStruct((features, wide), BF16),
        scratch_shapes=[pltpu.VMEM((features, tokens), BF16)],
        compiler_params=PARAMS,
        cost_estimate=SMALL,
    )(mine, grads, packet, got)


def swap_in(part, distance, axis):
    theirs = lax.ppermute(part, axis, [(i, i ^ distance) for i in range(lax.axis_size(axis))])
    low = lax.rem(lax.axis_index(axis) // distance, 2) == 0
    return jnp.where(low, jnp.concatenate([part, theirs]), jnp.concatenate([theirs, part]))


class Line:
    def __init__(self, token):
        self.token = token

    def arrived(self, *values):
        *values, self.token = lax.optimization_barrier((*values, self.token))
        return values if len(values) > 1 else values[0]

    def meet(self, chains, *values):
        flat = [array for chain in chains for array in chain.flying]
        flat = lax.optimization_barrier((*flat, *values, self.token))
        at = 0
        for chain in chains:
            chain.flying = list(flat[at : at + len(chain.flying)])
            at += len(chain.flying)
        self.token = flat[-1]
        return flat[at:-1]


def local(layer_input, resid_grad, qkv_grad, prev_input, prev_qkv_grad, qkv_weight, norm_gain):
    axis = "fsdp"
    rows_now, resid, grads_now = layer_input[0], resid_grad[0], qkv_grad[0]
    rows_prev, grads_prev = prev_input[0], prev_qkv_grad[0]
    weight_rows, gain = qkv_weight[0], norm_gain[0]
    owned, columns = weight_rows.shape
    tokens = rows_now.shape[0]
    count = lax.axis_size(axis)
    pairs = count // 2
    me = lax.axis_index(axis)
    pair, side = me // 2, lax.rem(me, 2)
    first = side == 0
    layers = lax.axis_size("section")
    line = Line(gain)

    cuts = [0, columns // 2, columns]
    bounds = [0, tokens // 2, tokens]
    parts = [slice(bounds[i], bounds[i + 1]) for i in range(2)]

    def summing(i, got, got_start):
        term = weight_term(normed_mine, grads_prev, cuts[i], packet, got, got_start)
        return Scatter(term, axis, pairs, pair, owned)

    def toward(got):
        return transpose_product(got, weight_half, BF16)

    def up_a_layer(i, theirs):
        local_grad = input_gradient(
            direction_mine, theirs, bounds[i], rows_now, resid, line.token, side, owned
        )
        return lax.ppermute(local_grad, "section", [(k + 1, k) for k in range(layers - 1)])

    normed_mine, packet = first_packet(rows_prev, gain, grads_prev, cuts[1], side, owned)
    packet = swap(line.arrived(packet), axis)
    gather = Gather(line.arrived(weight_rows), axis, pairs, pair)
    x2 = swap(line.arrived(grads_prev)[:, cuts[1] :], axis)

    line.meet([gather])
    gather.advance()
    (packet,) = line.meet([], packet)
    sum0 = summing(0, packet, normed_mine.shape[0])
    g0 = swap(line.arrived(grads_now[parts[0]]), axis)
    line.meet([gather])
    gather.advance()
    line.meet([sum0])
    sum0.advance()
    g1 = swap(line.arrived(grads_now[parts[1]]), axis)
    (x2,) = line.meet([], x2)
    sum1 = summing(1, x2, 0)
    line.meet([sum0])
    sum0.advance()
    line.meet([gather])
    while not gather.done():
        gather.advance()
        line.meet([gather])
    weight_half = line.arrived(gather.whole())
    line.meet([sum1])
    sum1.advance()
    (g0,) = line.meet([], g0)
    r0 = swap(line.arrived(toward(g0)), axis)
    direction_mine = line.arrived(transpose_product(grads_now, weight_half, F32))
    line.meet([sum1])
    sum1.advance()
    (g1,) = line.meet([], g1)
    r1 = swap(line.arrived(toward(g1)), axis)
    r0 = line.arrived(r0)
    u0 = up_a_layer(0, r0)
    line.meet([sum0, sum1])
    for chain in (sum0, sum1):
        while not chain.done():
            chain.advance()
            line.meet([chain])
    weight_grad = jnp.concatenate([chain.total() for chain in (sum0, sum1)], axis=1)
    owned_gain = lax.dynamic_slice_in_dim(gain, me * owned, owned, 0)
    gain_part = jnp.sum(weight_rows.astype(F32) * weight_grad, axis=1) / owned_gain
    gain_grad = swap_in(gain_part, 1, axis)
    r1 = line.arrived(r1)
    u1 = up_a_layer(1, r1)
    distance = 2
    while distance < count:
        gain_grad = swap_in(gain_grad, distance, axis)
        distance *= 2
    upstream_grad = jnp.concatenate([u0, u1], axis=0)
    return (upstream_grad[None], weight_grad[None], gain_grad[None])


def solution(mesh):
    placed = (
        P("section", "fsdp", None),
        P("section", "fsdp", None),
        P("section", "fsdp", None),
        P("section", "fsdp", None),
        P("section", "fsdp", None),
        P("section", "fsdp", None),
        P("section", None),
    )
    return jax.shard_map(
        local,
        mesh=mesh,
        in_specs=placed,
        out_specs=(P("section", "fsdp", None), P("section", "fsdp", None), P("section", None)),
        check_vma=False,
    )
```

```python
import math

import jax
import jax.numpy as jnp
from jax import lax
from jax.experimental import pallas as pl
from jax.experimental.pallas import tpu as pltpu
from jax.sharding import PartitionSpec as P

EPS = 1e-05
BF16 = jnp.bfloat16
F32 = jnp.float32


def row_scale(rows):
    values = rows.astype(F32)
    return lax.rsqrt(jnp.mean(values * values, axis=-1, keepdims=True) + EPS)


def swap(value, axis):
    count = lax.axis_size(axis)
    return lax.ppermute(value, axis, [(i, i ^ 1) for i in range(count)])


def hop(value, axis, sources, step):
    return lax.ppermute(
        value, axis, [(2 * o + q, 2 * (o + step) + q) for o in sources for q in range(2)]
    )


def split_halves(array, owned):
    pieces = [array[..., i : i + owned] for i in range(0, array.shape[-1], owned)]
    return jnp.concatenate(pieces[0::2], axis=-1), jnp.concatenate(pieces[1::2], axis=-1)


def join_halves(even, odd, owned):
    pieces = []
    for i in range(0, even.shape[-1], owned):
        pieces += [even[..., i : i + owned], odd[..., i : i + owned]]
    return jnp.concatenate(pieces, axis=-1)


class Gather:
    def __init__(self, shard, axis, pairs, pair):
        self.shard, self.axis, self.pairs, self.pair = shard, axis, pairs, pair
        self.ups, self.downs, self.flying = [], [], []
        self.advance()

    def advance(self):
        if self.flying:
            self.ups.append(self.flying[0])
            self.downs.append(self.flying[1])
        r = len(self.ups) + 1
        up = hop(([self.shard] + self.ups)[-1], self.axis, range(r - 1, self.pairs - 1), 1)
        down = hop(([self.shard] + self.downs)[-1], self.axis, range(1, self.pairs - r + 1), -1)
        self.flying = [up, down]

    def done(self):
        return len(self.ups) == self.pairs - 2

    def whole(self):
        return assemble(self.pair, self.shard, self.ups + self.flying[:1], self.downs + self.flying[1:])


class Scatter:
    def __init__(self, term, axis, pairs, pair, owned, line):
        self.term, self.axis, self.pairs, self.pair, self.owned = term, axis, pairs, pair, owned
        self.line = line
        self.step, self.flying = 0, []
        self.advance()

    def advance(self):
        self.step += 1
        s, pairs, pair = self.step, self.pairs, self.pair
        above = jnp.minimum(pair + pairs - s, pairs - 1)
        below = jnp.maximum(pair - pairs + s, 0)
        if s == 1 and pairs >= 4:
            (send,) = pick_and_add(self.term, [jnp.where(pair < pairs // 2, above, below)], [], self.owned)
            route = [(q, 2 + q) for q in range(2)]
            route += [(2 * pairs - 2 + q, 2 * pairs - 4 + q) for q in range(2)]
            self.flying = [lax.ppermute(send, self.axis, route)]
            return
        came = [self.flying[0], self.flying[-1]] if self.flying else []
        send_up, send_down = self.line.arrived(*pick_and_add(self.term, [above, below], came, self.owned))
        self.flying = [
            hop(send_up, self.axis, range(s), 1),
            hop(send_down, self.axis, range(pairs - s, pairs), -1),
        ]

    def done(self):
        return self.step == self.pairs - 1


SMALL = pl.CostEstimate(flops=1, bytes_accessed=1, transcendentals=0)
VMEM = pl.BlockSpec(memory_space=pltpu.VMEM)
SMEM = pl.BlockSpec(memory_space=pltpu.SMEM)
ANY = pl.BlockSpec(memory_space=pl.ANY)
WHOLE = pltpu.CompilerParams(vmem_limit_bytes=60 * 1024 * 1024)
PARAMS = pltpu.CompilerParams(vmem_limit_bytes=24 * 1024 * 1024)


def assemble(pair, shard, ups, downs):
    pairs, owned = len(ups) + 1, shard.shape[0]

    def kernel(pair_ref, shard_ref, *refs):
        up_refs, down_refs = refs[: pairs - 1], refs[pairs - 1 : 2 * pairs - 2]
        out_ref, slots, came, gone = refs[2 * pairs - 2 :]
        here = pair_ref[0]

        def bring(source, at):
            return pltpu.make_async_copy(source, slots.at[at], came.at[at])

        def put(at):
            return pltpu.make_async_copy(slots.at[at], out_ref.at[pl.ds(at * owned, owned)], gone.at[at])

        for at in range(pairs):
            for source_pair in range(pairs):
                distance = source_pair - at
                if distance == 0:
                    source = shard_ref
                elif distance > 0:
                    source = up_refs[distance - 1]
                else:
                    source = down_refs[-distance - 1]

                @pl.when(here == source_pair)
                def _(source=source, at=at):
                    bring(source, at).start()

        for at in range(pairs):
            bring(shard_ref, at).wait()
            put(at).start()
        for at in range(pairs):
            put(at).wait()

    return pl.pallas_call(
        kernel,
        out_shape=jax.ShapeDtypeStruct((pairs * owned, shard.shape[1]), shard.dtype),
        in_specs=[pl.BlockSpec(memory_space=pltpu.SMEM)] + [pl.BlockSpec(memory_space=pl.ANY)] * (2 * pairs - 1),
        out_specs=pl.BlockSpec(memory_space=pl.ANY),
        scratch_shapes=[
            pltpu.VMEM((pairs,) + shard.shape, shard.dtype),
            pltpu.SemaphoreType.DMA((pairs,)),
            pltpu.SemaphoreType.DMA((pairs,)),
        ],
        compiler_params=PARAMS,
        cost_estimate=SMALL,
    )(pair.reshape(1), shard, *ups, *downs)


def first_packet(rows, gain, grads, wide, side, owned):
    tokens, features = rows.shape
    half = features // 2
    blocks = 4
    block = tokens // blocks

    def kernel(side_ref, gain_ref, rows_any, grads_any, mine_ref, packet_ref, rows_ref, sems):
        def bring(i):
            here = pl.ds(i * block, block)
            return pltpu.make_async_copy(rows_any.at[here], rows_ref.at[here], sems.at[i])

        beside = pltpu.make_async_copy(grads_any.at[:, :wide], packet_ref.at[:, half:], sems.at[blocks])
        for i in range(blocks):
            bring(i).start()
        beside.start()
        first = side_ref[0] == 0
        for i in range(blocks):
            bring(i).wait()
            here = slice(i * block, (i + 1) * block)
            values = rows_ref[here, :].astype(F32)
            scale = lax.rsqrt(jnp.mean(values * values, axis=-1, keepdims=True) + EPS)
            normed = (values * scale * gain_ref[...]).astype(BF16)
            even, odd = split_halves(normed, owned)
            mine_ref[:, here] = jnp.where(first, even, odd).T
            packet_ref[here, :half] = jnp.where(first, odd, even)
        beside.wait()

    return pl.pallas_call(
        kernel,
        in_specs=[SMEM, VMEM, ANY, ANY],
        out_specs=[VMEM, VMEM],
        out_shape=[
            jax.ShapeDtypeStruct((half, tokens), BF16),
            jax.ShapeDtypeStruct((tokens, half + wide), BF16),
        ],
        scratch_shapes=[pltpu.VMEM((tokens, features), BF16), pltpu.SemaphoreType.DMA((blocks + 1,))],
        compiler_params=WHOLE,
        cost_estimate=SMALL,
    )(side.reshape(1), gain[None, :], rows, grads)


def pick_and_add(term, places, came, owned):
    wide = term.shape[1]
    count = len(places)

    def kernel(at_ref, term_any, *refs):
        came_refs, out_refs = refs[: len(came)], refs[len(came) : len(came) + count]
        picked, sems = refs[len(came) + count :]
        copies = []
        for i in range(count):
            start = pl.multiple_of(at_ref[i] * owned, owned)
            target = picked.at[i] if came else out_refs[i]
            copies.append(pltpu.make_async_copy(term_any.at[pl.ds(start, owned)], target, sems.at[i]))
        for copy in copies:
            copy.start()
        for i, copy in enumerate(copies):
            copy.wait()
            if came:
                out_refs[i][...] = (picked[i].astype(F32) + came_refs[i][...].astype(F32)).astype(BF16)

    return pl.pallas_call(
        kernel,
        in_specs=[SMEM, ANY] + [VMEM] * len(came),
        out_specs=[VMEM] * count,
        out_shape=[jax.ShapeDtypeStruct((owned, wide), BF16)] * count,
        scratch_shapes=[pltpu.VMEM((count, owned, wide), BF16), pltpu.SemaphoreType.DMA((count,))],
        compiler_params=PARAMS,
        cost_estimate=SMALL,
    )(jnp.stack(places), term, *came)


def transpose_product(pieces, weight, dtype):
    features = weight.shape[0]
    rows = [piece.shape[0] for piece in pieces]
    block = min(256, features)

    def kernel(*refs):
        weight_ref, out_ref = refs[-2:]
        for i, piece_ref in enumerate(refs[:-2]):
            top = sum(rows[:i])
            for at in range(0, features, block):
                out_ref[top : top + rows[i], at : at + block] = lax.dot_general(
                    piece_ref[...], weight_ref[at : at + block, :], (((1,), (1,)), ((), ())),
                    preferred_element_type=F32,
                ).astype(dtype)

    return pl.pallas_call(
        kernel,
        in_specs=[VMEM] * (len(pieces) + 1),
        out_specs=VMEM,
        out_shape=jax.ShapeDtypeStruct((sum(rows), features), dtype),
        compiler_params=PARAMS,
        cost_estimate=SMALL,
    )(*pieces, weight)


def input_gradient(mine, theirs, start, rows, resid, gain, side, owned, cost):
    tokens, half = theirs.shape
    block = min(64, tokens)

    def kernel(side_ref, mine_ref, theirs_ref, rows_ref, resid_ref, gain_ref, out_ref):
        first = side_ref[0] == 0

        def part(i, carry):
            here = pl.ds(pl.multiple_of(i * block, block), block)
            mine_part = mine_ref[pl.ds(pl.multiple_of(start + i * block, block), block), :]
            theirs_part = theirs_ref[here, :].astype(F32)
            even = jnp.where(first, mine_part, theirs_part)
            odd = jnp.where(first, theirs_part, mine_part)
            values = rows_ref[here, :].astype(F32)
            scale = lax.rsqrt(jnp.mean(values * values, axis=-1, keepdims=True) + EPS)
            gained = gain_ref[...] * join_halves(even, odd, owned)
            inner = jnp.mean(gained * values, axis=-1, keepdims=True)
            out_ref[here, :] = (
                resid_ref[here, :].astype(F32) + scale * gained - values * (scale * scale * scale * inner)
            ).astype(BF16)
            return carry

        lax.fori_loop(0, tokens // block, part, 0)

    return pl.pallas_call(
        kernel,
        in_specs=[SMEM] + [VMEM] * 5,
        out_specs=VMEM,
        out_shape=jax.ShapeDtypeStruct((tokens, 2 * half), BF16),
        compiler_params=PARAMS,
        cost_estimate=cost,
    )(side.reshape(1), mine, theirs, rows, resid, gain[None, :])


def owned_sums(chains, weight_rows, pair, owned):
    each = [[chain.term, *chain.flying] for chain in chains]
    came = [array for arrays in each for array in arrays[1:]]
    wides = [arrays[0].shape[1] for arrays in each]

    def kernel(pair_ref, weight_any, *refs):
        terms, came_refs = refs[: len(each)], refs[len(each) : len(each) + len(came)]
        total_ref, part_ref = refs[len(each) + len(came) :][:2]
        own_refs, (weight_ref, sems) = refs[len(each) + len(came) + 2 : -2], refs[-2:]
        start = pl.multiple_of(pair_ref[0] * owned, owned)
        copies = [
            pltpu.make_async_copy(terms[i].at[pl.ds(start, owned)], own_refs[i], sems.at[i]) for i in range(len(each))
        ]
        copies.append(pltpu.make_async_copy(weight_any, weight_ref, sems.at[len(each)]))
        for copy in copies:
            copy.start()
        for copy in copies:
            copy.wait()
        along = jnp.zeros((owned, 128), F32)
        column = at = 0
        for i, arrays in enumerate(each):
            for left in range(0, wides[i], 128):
                here = slice(left, left + 128)
                total = own_refs[i][:, here].astype(F32)
                for k in range(len(arrays) - 1):
                    total = total + came_refs[at + k][:, here].astype(F32)
                total_ref[:, column : column + 128] = total
                along = along + weight_ref[:, column : column + 128].astype(F32) * total
                column += 128
            at += len(arrays) - 1
        part_ref[...] = jnp.sum(along.T, axis=0, keepdims=True)

    return pl.pallas_call(
        kernel,
        in_specs=[SMEM, ANY] + [ANY] * len(each) + [VMEM] * len(came),
        out_specs=[VMEM, VMEM],
        out_shape=[jax.ShapeDtypeStruct((owned, sum(wides)), F32), jax.ShapeDtypeStruct((1, owned), F32)],
        scratch_shapes=[pltpu.VMEM((owned, wide), BF16) for wide in wides]
        + [pltpu.VMEM(weight_rows.shape, BF16), pltpu.SemaphoreType.DMA((len(each) + 1,))],
        compiler_params=PARAMS,
        cost_estimate=SMALL,
    )(pair.reshape(1), weight_rows, *[arrays[0] for arrays in each], *came)


def weight_term(mine, theirs, grads, start, got, got_start):
    features, tokens = mine.shape
    wide = got.shape[1] - got_start
    block = math.gcd(512, wide)
    fresh = theirs is None

    def kernel(mine_any, grads_any, got_any, *refs):
        theirs_any = got_any.at[:, :features] if fresh else refs[0]
        out_ref, mine_ref, grads_ref, got_ref, theirs_ref, sems = refs[-6:]
        copies = [
            pltpu.make_async_copy(theirs_any, theirs_ref, sems.at[0]),
            pltpu.make_async_copy(mine_any, mine_ref, sems.at[1]),
            pltpu.make_async_copy(grads_any.at[:, start : start + wide], grads_ref, sems.at[2]),
            pltpu.make_async_copy(got_any.at[:, got_start : got_start + wide], got_ref, sems.at[3]),
        ]
        for copy in copies:
            copy.start()
        copies[0].wait()
        if fresh:
            flipped = refs[0]
            flipped[...] = theirs_ref[...].T
        else:
            flipped = theirs_ref
        for copy in copies[1:]:
            copy.wait()
        for at in range(0, wide, block):
            total = jnp.dot(mine_ref[...], grads_ref[:, at : at + block], preferred_element_type=F32)
            total += jnp.dot(flipped[...], got_ref[:, at : at + block], preferred_element_type=F32)
            out_ref[:, at : at + block] = total.astype(BF16)

    out_shape = [jax.ShapeDtypeStruct((features, wide), BF16)]
    if fresh:
        out_shape.insert(0, jax.ShapeDtypeStruct((features, tokens), BF16))
    operands = [mine, grads, got] + ([] if fresh else [theirs])
    outs = pl.pallas_call(
        kernel,
        in_specs=[ANY] * len(operands),
        out_specs=[VMEM] * len(out_shape),
        out_shape=out_shape,
        scratch_shapes=[
            pltpu.VMEM((features, tokens), BF16),
            pltpu.VMEM((tokens, wide), BF16),
            pltpu.VMEM((tokens, wide), BF16),
            pltpu.VMEM((tokens, features) if fresh else (features, tokens), BF16),
            pltpu.SemaphoreType.DMA((4,)),
        ],
        compiler_params=PARAMS,
        cost_estimate=SMALL,
    )(*operands)
    return outs if fresh else (theirs, outs[0])


class Line:
    def __init__(self, token):
        self.token = token

    def arrived(self, *values):
        *values, self.token = lax.optimization_barrier((*values, self.token))
        return values if len(values) > 1 else values[0]

    def meet(self, chains, *values):
        flat = [array for chain in chains for array in chain.flying]
        flat = lax.optimization_barrier((*flat, *values, self.token))
        at = 0
        for chain in chains:
            chain.flying = list(flat[at : at + len(chain.flying)])
            at += len(chain.flying)
        self.token = flat[-1]
        return flat[at:-1]


def local(layer_input, resid_grad, qkv_grad, prev_input, prev_qkv_grad, qkv_weight, norm_gain):
    axis = "fsdp"
    rows_now, resid, grads_now = layer_input[0], resid_grad[0], qkv_grad[0]
    rows_prev, grads_prev = prev_input[0], prev_qkv_grad[0]
    weight_rows, gain = qkv_weight[0], norm_gain[0]
    owned, columns = weight_rows.shape
    tokens = rows_now.shape[0]
    count = lax.axis_size(axis)
    pairs = count // 2
    me = lax.axis_index(axis)
    pair, side = me // 2, lax.rem(me, 2)
    first = side == 0
    layers = lax.axis_size("section")
    line = Line(gain)

    cuts = [0, columns * 5 // 12, columns]
    bounds = [0, tokens // 2, tokens]

    def summing(term):
        return Scatter(term, axis, pairs, pair, owned, line)

    helped, stands_in = 2, lax.axis_index("section") == 0
    layer_list = list(range(layers))

    def to_stand_in(own):
        return lax.ppermute(own, "section", [(helped, 0)])

    def swap_in_layers(value, idle):
        return lax.ppermute(
            value,
            ("section", axis),
            [(k * count + i, k * count + (i ^ 1)) for k in layer_list if k != idle for i in range(count)],
        )

    def back(piece, idle):
        return swap_in_layers(line.arrived(transpose_product([piece], weight_half, BF16)), idle)

    def up_a_layer(i, theirs, cost=SMALL):
        rows, resid, gain_of = part_inputs[i]
        local_grad = line.arrived(
            input_gradient(direction_mine, theirs, bounds[i], rows, resid, gain_of, side, owned, cost)
        )
        route = [(k, k - 1) for k in layer_list[1:]]
        if i == 1:
            route = [(0 if k == helped else k, k - 1) for k in layer_list[1:]]
        return lax.ppermute(local_grad, "section", route)

    normed_mine, packet = first_packet(rows_prev, gain, grads_prev, cuts[1], side, owned)
    packet = swap(line.arrived(packet), axis)
    weight_there, gain_there = line.arrived(to_stand_in(weight_rows), to_stand_in(gain))
    gather = Gather(jnp.where(stands_in, weight_there, weight_rows), axis, pairs, pair)
    gain_second = jnp.where(stands_in, gain_there, gain)
    seconds = [grads_now[bounds[1] :], rows_now[bounds[1] :], resid[bounds[1] :]]
    there = to_stand_in(jnp.concatenate(seconds, axis=1))
    x2 = swap(line.arrived(grads_prev)[:, cuts[1] :], axis)

    line.meet([gather])
    gather.advance()
    (packet,) = line.meet([], packet)
    normed_theirs, term0 = weight_term(normed_mine, None, grads_prev, cuts[0], packet, normed_mine.shape[0])
    sum0 = summing(term0)
    now_first = line.arrived(grads_now[: bounds[1]])
    g0 = swap_in_layers(now_first, 0)
    line.meet([gather])
    gather.advance()
    line.meet([sum0])
    sum0.advance()
    x2, there = line.meet([], x2, there)
    edges = [0, columns, columns + rows_now.shape[1], there.shape[1]]
    now_second, rows_second, resid_second = [
        jnp.where(stands_in, there[:, edges[i] : edges[i + 1]], seconds[i]) for i in range(3)
    ]
    g1 = swap_in_layers(line.arrived(now_second), helped)
    unused, term1 = weight_term(normed_mine, normed_theirs, grads_prev, cuts[1], x2, 0)
    sum1 = summing(term1)
    line.meet([sum0])
    sum0.advance()
    line.meet([gather])
    while not gather.done():
        gather.advance()
        line.meet([gather])
    weight_half = gather.whole()
    direction_mine = line.arrived(transpose_product([now_first, now_second], weight_half, F32))
    part_inputs = [(rows_now[: bounds[1]], resid[: bounds[1]], gain), (rows_second, resid_second, gain_second)]
    line.meet([sum1])
    sum1.advance()
    (g0,) = line.meet([], g0)
    r0 = back(g0, 0)
    line.meet([sum1])
    sum1.advance()
    (g1,) = line.meet([], g1)
    r1 = back(g1, helped)
    line.meet([sum0])
    r0 = line.arrived(r0)
    u0 = up_a_layer(0, r0)
    r1 = line.arrived(r1)
    u1 = up_a_layer(1, r1)
    line.meet([sum0, sum1])
    for chain in (sum0, sum1):
        while not chain.done():
            chain.advance()
            line.meet([chain])
    weight_grad, gain_part = owned_sums((sum0, sum1), weight_rows, pair, owned)
    gain_grad = line.arrived(gain_part)[0]
    there = line.arrived(swap(gain_grad, axis))
    gain_grad = jnp.where(first, jnp.concatenate([gain_grad, there]), jnp.concatenate([there, gain_grad]))
    others = [
        lax.ppermute(gain_grad, axis, [(i, (i + 2 * k) % count) for i in range(count)]) for k in range(1, pairs)
    ]
    u0, u1 = line.arrived(u0, u1)
    upstream_grad = line.arrived(jnp.concatenate([u0, u1], axis=0))
    features = jnp.stack([gain_grad, *line.arrived(*others)])
    gain_grad = features[lax.rem(pair - jnp.arange(pairs) + pairs, pairs)].reshape(-1) / line.token
    return (upstream_grad[None], weight_grad[None], gain_grad[None])


def solution(mesh):
    placed = (
        P("section", "fsdp", None),
        P("section", "fsdp", None),
        P("section", "fsdp", None),
        P("section", "fsdp", None),
        P("section", "fsdp", None),
        P("section", "fsdp", None),
        P("section", None),
    )
    return jax.shard_map(
        local,
        mesh=mesh,
        in_specs=placed,
        out_specs=(P("section", "fsdp", None), P("section", "fsdp", None), P("section", None)),
        check_vma=False,
    )
```

```python
import math

import jax
import jax.numpy as jnp
from jax import lax
from jax.experimental import pallas as pl
from jax.experimental.pallas import tpu as pltpu
from jax.sharding import PartitionSpec as P

EPS = 1e-05
BF16 = jnp.bfloat16
F32 = jnp.float32


def row_scale(rows):
    values = rows.astype(F32)
    return lax.rsqrt(jnp.mean(values * values, axis=-1, keepdims=True) + EPS)


def swap(value, axis):
    count = lax.axis_size(axis)
    return lax.ppermute(value, axis, [(i, i ^ 1) for i in range(count)])


def hop(value, axis, sources, step):
    return lax.ppermute(
        value, axis, [(2 * o + q, 2 * (o + step) + q) for o in sources for q in range(2)]
    )


def split_halves(array, owned):
    pieces = [array[..., i : i + owned] for i in range(0, array.shape[-1], owned)]
    return jnp.concatenate(pieces[0::2], axis=-1), jnp.concatenate(pieces[1::2], axis=-1)


def join_halves(even, odd, owned):
    pieces = []
    for i in range(0, even.shape[-1], owned):
        pieces += [even[..., i : i + owned], odd[..., i : i + owned]]
    return jnp.concatenate(pieces, axis=-1)


class Gather:
    def __init__(self, shard, axis, pairs, pair):
        self.shard, self.axis, self.pairs, self.pair = shard, axis, pairs, pair
        self.ups, self.downs, self.flying = [], [], []
        self.advance()

    def advance(self):
        if self.flying:
            self.ups.append(self.flying[0])
            self.downs.append(self.flying[1])
        r = len(self.ups) + 1
        up = hop(([self.shard] + self.ups)[-1], self.axis, range(r - 1, self.pairs - 1), 1)
        down = hop(([self.shard] + self.downs)[-1], self.axis, range(1, self.pairs - r + 1), -1)
        self.flying = [up, down]

    def done(self):
        return len(self.ups) == self.pairs - 2

    def whole(self):
        return assemble(self.pair, self.shard, self.ups + self.flying[:1], self.downs + self.flying[1:])


class Scatter:
    def __init__(self, term, axis, pairs, pair, owned, line):
        self.term, self.axis, self.pairs, self.pair, self.owned = term, axis, pairs, pair, owned
        self.line = line
        self.step, self.flying = 0, []
        self.advance()

    def advance(self):
        self.step += 1
        s, pairs, pair = self.step, self.pairs, self.pair
        above = jnp.minimum(pair + pairs - s, pairs - 1)
        below = jnp.maximum(pair - pairs + s, 0)
        if s == 1 and pairs >= 4:
            (send,) = pick_and_add(self.term, [jnp.where(pair < pairs // 2, above, below)], [], self.owned)
            route = [(q, 2 + q) for q in range(2)]
            route += [(2 * pairs - 2 + q, 2 * pairs - 4 + q) for q in range(2)]
            self.flying = [lax.ppermute(send, self.axis, route)]
            return
        came = [self.flying[0], self.flying[-1]] if self.flying else []
        send_up, send_down = self.line.arrived(*pick_and_add(self.term, [above, below], came, self.owned))
        self.flying = [
            hop(send_up, self.axis, range(s), 1),
            hop(send_down, self.axis, range(pairs - s, pairs), -1),
        ]

    def done(self):
        return self.step == self.pairs - 1


SMALL = pl.CostEstimate(flops=1, bytes_accessed=1, transcendentals=0)
VMEM = pl.BlockSpec(memory_space=pltpu.VMEM)
SMEM = pl.BlockSpec(memory_space=pltpu.SMEM)
ANY = pl.BlockSpec(memory_space=pl.ANY)
WHOLE = pltpu.CompilerParams(vmem_limit_bytes=60 * 1024 * 1024)
PARAMS = pltpu.CompilerParams(vmem_limit_bytes=24 * 1024 * 1024)


def assemble(pair, shard, ups, downs):
    pairs, owned = len(ups) + 1, shard.shape[0]

    def kernel(pair_ref, shard_ref, *refs):
        up_refs, down_refs = refs[: pairs - 1], refs[pairs - 1 : 2 * pairs - 2]
        out_ref, slots, came, gone = refs[2 * pairs - 2 :]
        here = pair_ref[0]

        def bring(source, at):
            return pltpu.make_async_copy(source, slots.at[at], came.at[at])

        def put(at):
            return pltpu.make_async_copy(slots.at[at], out_ref.at[pl.ds(at * owned, owned)], gone.at[at])

        for at in range(pairs):
            for source_pair in range(pairs):
                distance = source_pair - at
                if distance == 0:
                    source = shard_ref
                elif distance > 0:
                    source = up_refs[distance - 1]
                else:
                    source = down_refs[-distance - 1]

                @pl.when(here == source_pair)
                def _(source=source, at=at):
                    bring(source, at).start()

        for at in range(pairs):
            bring(shard_ref, at).wait()
            put(at).start()
        for at in range(pairs):
            put(at).wait()

    return pl.pallas_call(
        kernel,
        out_shape=jax.ShapeDtypeStruct((pairs * owned, shard.shape[1]), shard.dtype),
        in_specs=[pl.BlockSpec(memory_space=pltpu.SMEM)] + [pl.BlockSpec(memory_space=pl.ANY)] * (2 * pairs - 1),
        out_specs=pl.BlockSpec(memory_space=pl.ANY),
        scratch_shapes=[
            pltpu.VMEM((pairs,) + shard.shape, shard.dtype),
            pltpu.SemaphoreType.DMA((pairs,)),
            pltpu.SemaphoreType.DMA((pairs,)),
        ],
        compiler_params=PARAMS,
        cost_estimate=SMALL,
    )(pair.reshape(1), shard, *ups, *downs)


def first_packet(rows, gain, grads, wide, side, owned):
    tokens, features = rows.shape
    half = features // 2
    blocks = 4
    block = tokens // blocks

    def kernel(side_ref, gain_ref, rows_any, grads_any, mine_ref, packet_ref, rows_ref, sems):
        def bring(i):
            here = pl.ds(i * block, block)
            return pltpu.make_async_copy(rows_any.at[here], rows_ref.at[here], sems.at[i])

        beside = pltpu.make_async_copy(grads_any.at[:, :wide], packet_ref.at[:, half:], sems.at[blocks])
        for i in range(blocks):
            bring(i).start()
        beside.start()
        first = side_ref[0] == 0
        for i in range(blocks):
            bring(i).wait()
            here = slice(i * block, (i + 1) * block)
            values = rows_ref[here, :].astype(F32)
            scale = lax.rsqrt(jnp.mean(values * values, axis=-1, keepdims=True) + EPS)
            normed = (values * scale * gain_ref[...]).astype(BF16)
            even, odd = split_halves(normed, owned)
            mine_ref[:, here] = jnp.where(first, even, odd).T
            packet_ref[here, :half] = jnp.where(first, odd, even)
        beside.wait()

    return pl.pallas_call(
        kernel,
        in_specs=[SMEM, VMEM, ANY, ANY],
        out_specs=[VMEM, VMEM],
        out_shape=[
            jax.ShapeDtypeStruct((half, tokens), BF16),
            jax.ShapeDtypeStruct((tokens, half + wide), BF16),
        ],
        scratch_shapes=[pltpu.VMEM((tokens, features), BF16), pltpu.SemaphoreType.DMA((blocks + 1,))],
        compiler_params=WHOLE,
        cost_estimate=SMALL,
    )(side.reshape(1), gain[None, :], rows, grads)


def pick_and_add(term, places, came, owned):
    wide = term.shape[1]
    count = len(places)

    def kernel(at_ref, term_any, *refs):
        came_refs, out_refs = refs[: len(came)], refs[len(came) : len(came) + count]
        picked, sems = refs[len(came) + count :]
        copies = []
        for i in range(count):
            start = pl.multiple_of(at_ref[i] * owned, owned)
            target = picked.at[i] if came else out_refs[i]
            copies.append(pltpu.make_async_copy(term_any.at[pl.ds(start, owned)], target, sems.at[i]))
        for copy in copies:
            copy.start()
        for i, copy in enumerate(copies):
            copy.wait()
            if came:
                out_refs[i][...] = (picked[i].astype(F32) + came_refs[i][...].astype(F32)).astype(BF16)

    return pl.pallas_call(
        kernel,
        in_specs=[SMEM, ANY] + [VMEM] * len(came),
        out_specs=[VMEM] * count,
        out_shape=[jax.ShapeDtypeStruct((owned, wide), BF16)] * count,
        scratch_shapes=[pltpu.VMEM((count, owned, wide), BF16), pltpu.SemaphoreType.DMA((count,))],
        compiler_params=PARAMS,
        cost_estimate=SMALL,
    )(jnp.stack(places), term, *came)


def transpose_product(pieces, weight, dtype):
    features = weight.shape[0]
    rows = [piece.shape[0] for piece in pieces]
    block = min(256, features)

    def kernel(*refs):
        weight_ref, out_ref = refs[-2:]
        for i, piece_ref in enumerate(refs[:-2]):
            top = sum(rows[:i])
            for at in range(0, features, block):
                out_ref[top : top + rows[i], at : at + block] = lax.dot_general(
                    piece_ref[...], weight_ref[at : at + block, :], (((1,), (1,)), ((), ())),
                    preferred_element_type=F32,
                ).astype(dtype)

    return pl.pallas_call(
        kernel,
        in_specs=[VMEM] * (len(pieces) + 1),
        out_specs=VMEM,
        out_shape=jax.ShapeDtypeStruct((sum(rows), features), dtype),
        compiler_params=PARAMS,
        cost_estimate=SMALL,
    )(*pieces, weight)


def input_gradient(mine, theirs, start, rows, resid, gain, side, owned, cost):
    tokens, half = theirs.shape
    block = min(64, tokens)

    def kernel(side_ref, mine_ref, theirs_ref, rows_ref, resid_ref, gain_ref, out_ref):
        first = side_ref[0] == 0

        def part(i, carry):
            here = pl.ds(pl.multiple_of(i * block, block), block)
            mine_part = mine_ref[pl.ds(pl.multiple_of(start + i * block, block), block), :]
            theirs_part = theirs_ref[here, :].astype(F32)
            even = jnp.where(first, mine_part, theirs_part)
            odd = jnp.where(first, theirs_part, mine_part)
            values = rows_ref[here, :].astype(F32)
            scale = lax.rsqrt(jnp.mean(values * values, axis=-1, keepdims=True) + EPS)
            gained = gain_ref[...] * join_halves(even, odd, owned)
            inner = jnp.mean(gained * values, axis=-1, keepdims=True)
            out_ref[here, :] = (
                resid_ref[here, :].astype(F32) + scale * gained - values * (scale * scale * scale * inner)
            ).astype(BF16)
            return carry

        lax.fori_loop(0, tokens // block, part, 0)

    return pl.pallas_call(
        kernel,
        in_specs=[SMEM] + [VMEM] * 5,
        out_specs=VMEM,
        out_shape=jax.ShapeDtypeStruct((tokens, 2 * half), BF16),
        compiler_params=PARAMS,
        cost_estimate=cost,
    )(side.reshape(1), mine, theirs, rows, resid, gain[None, :])


def owned_sums(chains, weight_rows, pair, owned):
    each = [[chain.term, *chain.flying] for chain in chains]
    came = [array for arrays in each for array in arrays[1:]]
    wides = [arrays[0].shape[1] for arrays in each]

    def kernel(pair_ref, weight_any, *refs):
        terms, came_refs = refs[: len(each)], refs[len(each) : len(each) + len(came)]
        total_ref, part_ref = refs[len(each) + len(came) :][:2]
        own_refs, (weight_ref, sems) = refs[len(each) + len(came) + 2 : -2], refs[-2:]
        start = pl.multiple_of(pair_ref[0] * owned, owned)
        copies = [
            pltpu.make_async_copy(terms[i].at[pl.ds(start, owned)], own_refs[i], sems.at[i]) for i in range(len(each))
        ]
        copies.append(pltpu.make_async_copy(weight_any, weight_ref, sems.at[len(each)]))
        for copy in copies:
            copy.start()
        for copy in copies:
            copy.wait()
        along = jnp.zeros((owned, 128), F32)
        column = at = 0
        for i, arrays in enumerate(each):
            for left in range(0, wides[i], 128):
                here = slice(left, left + 128)
                total = own_refs[i][:, here].astype(F32)
                for k in range(len(arrays) - 1):
                    total = total + came_refs[at + k][:, here].astype(F32)
                total_ref[:, column : column + 128] = total
                along = along + weight_ref[:, column : column + 128].astype(F32) * total
                column += 128
            at += len(arrays) - 1
        part_ref[...] = jnp.sum(along.T, axis=0, keepdims=True)

    return pl.pallas_call(
        kernel,
        in_specs=[SMEM, ANY] + [ANY] * len(each) + [VMEM] * len(came),
        out_specs=[VMEM, VMEM],
        out_shape=[jax.ShapeDtypeStruct((owned, sum(wides)), F32), jax.ShapeDtypeStruct((1, owned), F32)],
        scratch_shapes=[pltpu.VMEM((owned, wide), BF16) for wide in wides]
        + [pltpu.VMEM(weight_rows.shape, BF16), pltpu.SemaphoreType.DMA((len(each) + 1,))],
        compiler_params=PARAMS,
        cost_estimate=SMALL,
    )(pair.reshape(1), weight_rows, *[arrays[0] for arrays in each], *came)


def weight_term(mine, theirs, grads, start, got, got_start):
    features, tokens = mine.shape
    wide = got.shape[1] - got_start
    block = math.gcd(512, wide)
    fresh = theirs is None

    def kernel(mine_any, grads_any, got_any, *refs):
        theirs_any = got_any.at[:, :features] if fresh else refs[0]
        out_ref, mine_ref, grads_ref, got_ref, theirs_ref, sems = refs[-6:]
        copies = [
            pltpu.make_async_copy(theirs_any, theirs_ref, sems.at[0]),
            pltpu.make_async_copy(mine_any, mine_ref, sems.at[1]),
            pltpu.make_async_copy(grads_any.at[:, start : start + wide], grads_ref, sems.at[2]),
            pltpu.make_async_copy(got_any.at[:, got_start : got_start + wide], got_ref, sems.at[3]),
        ]
        for copy in copies:
            copy.start()
        copies[0].wait()
        if fresh:
            flipped = refs[0]
            flipped[...] = theirs_ref[...].T
        else:
            flipped = theirs_ref
        for copy in copies[1:]:
            copy.wait()
        for at in range(0, wide, block):
            total = jnp.dot(mine_ref[...], grads_ref[:, at : at + block], preferred_element_type=F32)
            total += jnp.dot(flipped[...], got_ref[:, at : at + block], preferred_element_type=F32)
            out_ref[:, at : at + block] = total.astype(BF16)

    out_shape = [jax.ShapeDtypeStruct((features, wide), BF16)]
    if fresh:
        out_shape.insert(0, jax.ShapeDtypeStruct((features, tokens), BF16))
    operands = [mine, grads, got] + ([] if fresh else [theirs])
    outs = pl.pallas_call(
        kernel,
        in_specs=[ANY] * len(operands),
        out_specs=[VMEM] * len(out_shape),
        out_shape=out_shape,
        scratch_shapes=[
            pltpu.VMEM((features, tokens), BF16),
            pltpu.VMEM((tokens, wide), BF16),
            pltpu.VMEM((tokens, wide), BF16),
            pltpu.VMEM((tokens, features) if fresh else (features, tokens), BF16),
            pltpu.SemaphoreType.DMA((4,)),
        ],
        compiler_params=PARAMS,
        cost_estimate=SMALL,
    )(*operands)
    return outs if fresh else (theirs, outs[0])


class Line:
    def __init__(self, token):
        self.token = token

    def arrived(self, *values):
        *values, self.token = lax.optimization_barrier((*values, self.token))
        return values if len(values) > 1 else values[0]

    def meet(self, chains, *values):
        flat = [array for chain in chains for array in chain.flying]
        flat = lax.optimization_barrier((*flat, *values, self.token))
        at = 0
        for chain in chains:
            chain.flying = list(flat[at : at + len(chain.flying)])
            at += len(chain.flying)
        self.token = flat[-1]
        return flat[at:-1]


def local(layer_input, resid_grad, qkv_grad, prev_input, prev_qkv_grad, qkv_weight, norm_gain):
    axis = "fsdp"
    rows_now, resid, grads_now = layer_input[0], resid_grad[0], qkv_grad[0]
    rows_prev, grads_prev = prev_input[0], prev_qkv_grad[0]
    weight_rows, gain = qkv_weight[0], norm_gain[0]
    owned, columns = weight_rows.shape
    tokens = rows_now.shape[0]
    count = lax.axis_size(axis)
    pairs = count // 2
    me = lax.axis_index(axis)
    pair, side = me // 2, lax.rem(me, 2)
    first = side == 0
    layers = lax.axis_size("section")
    line = Line(gain)

    cuts = [0, columns * 5 // 12, columns]
    bounds = [0, tokens // 2, tokens]

    def summing(term):
        return Scatter(term, axis, pairs, pair, owned, line)

    helped, stands_in = 2, lax.axis_index("section") == 0
    layer_list = list(range(layers))

    def to_stand_in(own):
        return lax.ppermute(own, "section", [(helped, 0)])

    def swap_in_layers(value, idle):
        return lax.ppermute(
            value,
            ("section", axis),
            [(k * count + i, k * count + (i ^ 1)) for k in layer_list if k != idle for i in range(count)],
        )

    def back(piece, idle):
        return swap_in_layers(line.arrived(transpose_product([piece], weight_half, BF16)), idle)

    def up_a_layer(i, theirs, cost=SMALL):
        rows, resid, gain_of = part_inputs[i]
        local_grad = line.arrived(
            input_gradient(direction_mine, theirs, bounds[i], rows, resid, gain_of, side, owned, cost)
        )
        route = [(k, k - 1) for k in layer_list[1:]]
        if i == 1:
            route = [(0 if k == helped else k, k - 1) for k in layer_list[1:]]
        return lax.ppermute(local_grad, "section", route)

    normed_mine, packet = first_packet(rows_prev, gain, grads_prev, cuts[1], side, owned)
    packet = swap(line.arrived(packet), axis)
    weight_there, gain_there = line.arrived(to_stand_in(weight_rows), to_stand_in(gain))
    gather = Gather(jnp.where(stands_in, weight_there, weight_rows), axis, pairs, pair)
    gain_second = jnp.where(stands_in, gain_there, gain)
    seconds = [grads_now[bounds[1] :], rows_now[bounds[1] :], resid[bounds[1] :]]
    there = to_stand_in(jnp.concatenate(seconds, axis=1))
    x2 = swap(line.arrived(grads_prev)[:, cuts[1] :], axis)

    line.meet([gather])
    gather.advance()
    (packet,) = line.meet([], packet)
    normed_theirs, term0 = weight_term(normed_mine, None, grads_prev, cuts[0], packet, normed_mine.shape[0])
    sum0 = summing(term0)
    now_first = line.arrived(grads_now[: bounds[1]])
    g0 = swap_in_layers(now_first, 0)
    line.meet([gather])
    gather.advance()
    line.meet([sum0])
    sum0.advance()
    x2, there = line.meet([], x2, there)
    edges = [0, columns, columns + rows_now.shape[1], there.shape[1]]
    now_second, rows_second, resid_second = [
        jnp.where(stands_in, there[:, edges[i] : edges[i + 1]], seconds[i]) for i in range(3)
    ]
    g1 = swap_in_layers(line.arrived(now_second), helped)
    unused, term1 = weight_term(normed_mine, normed_theirs, grads_prev, cuts[1], x2, 0)
    sum1 = summing(term1)
    line.meet([sum0])
    sum0.advance()
    line.meet([gather])
    while not gather.done():
        gather.advance()
        line.meet([gather])
    weight_half = gather.whole()
    part_inputs = [(rows_now[: bounds[1]], resid[: bounds[1]], gain), (rows_second, resid_second, gain_second)]
    line.meet([sum1])
    sum1.advance()
    direction_mine = line.arrived(transpose_product([now_first, now_second], weight_half, F32))
    (g0,) = line.meet([], g0)
    r0 = back(g0, 0)
    line.meet([sum1])
    sum1.advance()
    (g1,) = line.meet([], g1)
    r1 = back(g1, helped)
    line.meet([sum0])
    r0 = line.arrived(r0)
    u0 = up_a_layer(0, r0)
    r1 = line.arrived(r1)
    u1 = up_a_layer(1, r1)
    line.meet([sum0, sum1])
    for chain in (sum0, sum1):
        while not chain.done():
            chain.advance()
            line.meet([chain])
    weight_grad, gain_part = owned_sums((sum0, sum1), weight_rows, pair, owned)
    gain_grad = line.arrived(gain_part)[0]
    there = line.arrived(swap(gain_grad, axis))
    gain_grad = jnp.where(first, jnp.concatenate([gain_grad, there]), jnp.concatenate([there, gain_grad]))
    others = [
        lax.ppermute(gain_grad, axis, [(i, (i + 2 * k) % count) for i in range(count)]) for k in range(1, pairs)
    ]
    u0, u1 = line.arrived(u0, u1)
    upstream_grad = line.arrived(jnp.concatenate([u0, u1], axis=0))
    features = jnp.stack([gain_grad, *line.arrived(*others)])
    gain_grad = features[lax.rem(pair - jnp.arange(pairs) + pairs, pairs)].reshape(-1) / line.token
    return (upstream_grad[None], weight_grad[None], gain_grad[None])


def solution(mesh):
    placed = (
        P("section", "fsdp", None),
        P("section", "fsdp", None),
        P("section", "fsdp", None),
        P("section", "fsdp", None),
        P("section", "fsdp", None),
        P("section", "fsdp", None),
        P("section", None),
    )
    return jax.shard_map(
        local,
        mesh=mesh,
        in_specs=placed,
        out_specs=(P("section", "fsdp", None), P("section", "fsdp", None), P("section", None)),
        check_vma=False,
    )
```
